256 devices in a mesh: ctx: 64 (over y, x_hi, z), tp: 4 (over x_lo, core).
Axes of the slice: x: 4 (x_hi: 2, x_lo: 2; x = x_hi * 2 + x_lo), y: 4, z: 8, core: 2. Of those that a mesh axis runs over, the one named last changes fastest.
Arguments:
- projected: bfloat16 [32768, 3, 4096], P('ctx', None, 'tp'), may hold values from -6 to 6
- short_taps: float32 [3, 3, 4096], P(None, None, 'tp'), may hold values from -3.5 to 3.5
- filter_taps: float32 [4096, 128], P('tp'), may hold values from -0.75 to 0.75
- decay_rates: float32 [4096], P('tp'), may hold values from 0.002 to 0.1
- bypass_gain: float32 [4096], P('tp'), may hold values from -5 to 5
- out_weight: bfloat16 [4096, 8192], P('tp', 'ctx'), may hold values from -0.09375 to 0.09375
Outputs:
- block_out: bfloat16 [32768, 8192], P(('ctx', 'tp'))
The draws below stay inside these ranges and needn't reach their ends.
All inputs are finite; a program needn't handle non-finite values.
Results may differ from the reference program's by a relative error of at most 0.013.
Values may be sent and summed in bfloat16 or wider, within the bound.
No kernel may reach another device: no remote copies, remote signals or barrier semaphores. Data moves between devices by JAX's collectives and lax.ppermute only.
A program may use at most 192 MiB of HBM per device.

```python
import math
import jax
import jax.numpy as jnp
from jax import lax

D = 8192
C = 4096
FILT = 128
TOK_DEV = 512
TOKENS = 32768
N_CTX = 64
N_TP = 4


def draw_decay_rates(key, part):
    key = jax.random.fold_in(key, 11)
    values = jax.random.uniform(key, (C,), jnp.float32, math.log(0.002), math.log(0.1))
    return jnp.exp(values).astype(jnp.float32)


def steps_of(own_key, dims, split, low, high):
    level = 1.0
    for axis_at, parts in split:
        draws = jax.random.uniform(jax.random.fold_in(jax.random.fold_in(own_key, 6), axis_at), (parts,), jnp.float32, low / len(split), high / len(split))
        level = level * jnp.repeat(jnp.exp(draws), dims[axis_at] // parts).reshape((-1,) + (1,) * (len(dims) - 1 - axis_at))
    return level


def centred(own_key, extent, deviation, bound, shards=(), kind=jnp.bfloat16):
    loudness = steps_of(own_key, extent, shards, -0.22, 0.18) if shards else 1.0
    values = jax.random.normal(own_key, extent, jnp.float32) * deviation * loudness
    return jnp.minimum(jnp.maximum(values, -bound), bound).astype(kind)


def setup_inputs(seed: int = 0) -> dict:
    keys = jax.random.split(jax.random.key(seed), 7)
    return {
        "projected": centred(keys[0], (TOKENS, 3, C), 1.0, 6.0, ((0, 64), (2, 4))),
        "short_taps": centred(keys[1], (3, 3, C), 3 ** -0.5, 3.5, ((2, 4),), jnp.float32),
        "filter_taps": centred(keys[2], (C, FILT), 64 ** -0.5, 0.75, ((0, 4),), jnp.float32),
        "decay_rates": draw_decay_rates(jax.random.fold_in(keys[6], 71), 0),
        "bypass_gain": centred(keys[4], (C,), 1.0, 5.0, ((0, 4),), jnp.float32),
        "out_weight": centred(keys[5], (C, D), C ** -0.5, 0.09375, ((0, 4), (1, 64))),
    }


def featurize(raw_rows, short_taps, row_total):
    running = short_taps[0] * raw_rows[2:2 + row_total].astype(jnp.float32)
    running = running + short_taps[1] * raw_rows[1:1 + row_total].astype(jnp.float32)
    running = running + short_taps[2] * raw_rows[0:row_total].astype(jnp.float32)
    return running.astype(jnp.bfloat16)


def make_filter(filter_taps, decay_rates):
    tap_lags = jnp.arange(FILT).astype(jnp.float32)
    return (filter_taps * jnp.exp(-decay_rates[:, None] * tap_lags[None, :])).astype(jnp.bfloat16)


def toeplitz_conv(product, filter_bank):
    blocks = product.shape[0] // FILT
    channels = product.shape[1]
    group_size = math.gcd(channels, 64)
    groups = channels // group_size
    lag_table = jnp.arange(FILT)[:, None] - jnp.arange(FILT)[None, :]
    current = product.reshape(blocks, FILT, groups, group_size)
    earlier = jnp.concatenate([jnp.zeros((1, FILT, groups, group_size), jnp.bfloat16), current[:-1]], axis=0)
    kernels = filter_bank.astype(jnp.float32).reshape(groups, group_size, FILT)

    def one_group(packed):
        block_now, block_before, taps_group = packed
        near_table = jnp.where(lag_table[None] >= 0, taps_group[:, jnp.clip(lag_table, 0, FILT - 1)], 0.0)
        far_table = jnp.where(lag_table[None] < 0, taps_group[:, jnp.clip(lag_table + FILT, 0, FILT - 1)], 0.0)
        result = jnp.einsum("gim,bmg->big", near_table, block_now.astype(jnp.float32), precision=lax.Precision.HIGHEST)
        result = result + jnp.einsum("gim,bmg->big", far_table, block_before.astype(jnp.float32), precision=lax.Precision.HIGHEST)
        return result

    grouped = lax.map(one_group, (jnp.moveaxis(current, 2, 0), jnp.moveaxis(earlier, 2, 0), kernels))
    return jnp.moveaxis(grouped, 0, 2).reshape(blocks * FILT, channels)


def reference(projected, short_taps, filter_taps, decay_rates, bypass_gain, out_weight):
    row_total = projected.shape[0]
    padded = jnp.concatenate([jnp.zeros((2, 3, C), jnp.bfloat16), projected], axis=0)
    featured = featurize(padded, short_taps, row_total)
    product = (featured[:, 1].astype(jnp.float32) * featured[:, 2].astype(jnp.float32)).astype(jnp.bfloat16)
    filter_bank = make_filter(filter_taps, decay_rates)
    long_part = toeplitz_conv(product, filter_bank)
    gated = (featured[:, 0].astype(jnp.float32) * (long_part + bypass_gain * product.astype(jnp.float32))).astype(jnp.bfloat16)
    quarter = C // N_TP

    def one_block(block_rows):
        running = jnp.zeros((TOK_DEV, D), jnp.float32)
        for slot_index in range(N_TP):
            partial_value = jnp.dot(block_rows[:, slot_index * quarter:(slot_index + 1) * quarter],
                              out_weight[slot_index * quarter:(slot_index + 1) * quarter],
                              preferred_element_type=jnp.float32)
            running = running + lax.optimization_barrier(partial_value.astype(jnp.bfloat16)).astype(jnp.float32)
        return running.astype(jnp.bfloat16)

    outputs = lax.map(one_block, gated.reshape(N_CTX, TOK_DEV, C))
    return outputs.reshape(TOKENS, D)
```

```python
import functools

import jax
import jax.numpy as jnp
import ml_dtypes
import numpy as np
from jax import lax
from jax.experimental import pallas as pl
from jax.experimental.pallas import tpu as pltpu
from jax.sharding import Mesh
from jax.sharding import PartitionSpec as P

TOK = 512
CH = 1024
TAPS = 128
WIN = 256
LANES = 256
CELL = ("xh", "xl", "c")
F32, BF16 = jnp.float32, jnp.bfloat16


def two_halves(matrix):
    high = matrix.astype(ml_dtypes.bfloat16)
    low = (matrix - high.astype(np.float64)).astype(ml_dtypes.bfloat16)
    return high, low


@functools.lru_cache(maxsize=None)
def transform_matrices():
    at = np.arange(WIN)
    half = WIN // 2
    angle = 2 * np.pi * (np.outer(np.arange(half), at) % WIN) / WIN
    sine = -np.sin(angle)
    sine[0] = np.cos(np.pi * at)
    forward = np.concatenate([np.cos(angle), sine])
    scale = np.where(np.arange(half) == 0, 1.0, 2.0)[:, None] / WIN
    scale_im = np.where(np.arange(half) == 0, 1.0, 2.0)[:, None] / WIN
    inverse = np.concatenate([np.cos(angle) * scale, sine * scale_im]).T[half:]
    fh, fl = two_halves(forward)
    ih, il = two_halves(inverse)
    return np.concatenate([fh, fl]), np.concatenate([ih, ih, il], axis=1)


def rolled(x, steps):
    return pltpu.roll(x, steps % x.shape[0], 0)


def featurize(rows, taps, count):
    lead = rows.shape[0] - count
    one = rolled(rows, 1)[lead:]
    two = rolled(rows, 2)[lead:]
    return (taps[0] * rows[lead:] + taps[1] * one + taps[2] * two).astype(BF16)


def tail_kernel(x_ref, taps_ref, out_ref):
    start = TOK - TAPS - 16
    streams = []
    raw = []
    for s in range(3):
        rows = x_ref[s, start:TOK, :].astype(F32)
        raw.append(rows[-8:])
        if s:
            taps = [taps_ref[j, s : s + 1, :] for j in range(3)]
            streams.append(featurize(rows, taps, TAPS).astype(F32))
    out_ref[:TAPS, :] = (streams[0] * streams[1]).astype(BF16)
    row = lax.broadcasted_iota(jnp.int32, raw[0].shape, 0)
    packed = jnp.where(row < 2, rolled(raw[0], 2), jnp.where(row < 4, rolled(raw[1], 4), rolled(raw[2], 6)))
    out_ref[TAPS:, :] = jnp.concatenate([packed, jnp.zeros_like(packed)], axis=0).astype(BF16)


def tail_rows(x, taps):
    return pl.pallas_call(
        tail_kernel,
        grid=(2,),
        in_specs=[
            pl.BlockSpec((3, TOK, CH // 2), lambda i: (0, 0, i)),
            pl.BlockSpec((3, 3, CH // 2), lambda i: (0, 0, i)),
        ],
        out_specs=pl.BlockSpec((TAPS + 16, CH // 2), lambda i: (0, i)),
        out_shape=jax.ShapeDtypeStruct((TAPS + 16, CH), BF16),
        compiler_params=pltpu.CompilerParams(vmem_limit_bytes=32 << 20),
        cost_estimate=pl.CostEstimate(flops=4 * TAPS * CH, bytes_accessed=3 << 20, transcendentals=0),
    )(x, taps)


def mixer_kernel(x_ref, halo_ref, taps_ref, filt_ref, rate_ref, gain_ref, fwd_ref, inv_ref, out_ref, prod, query):
    dot = functools.partial(lax.dot_general, preferred_element_type=F32)
    plain = (((1,), (0,)), ((), ()))
    half = WIN // 2

    lag = lax.broadcasted_iota(jnp.int32, (LANES, TAPS), 1).astype(F32)
    bank = (filt_ref[...] * jnp.exp(-rate_ref[...] * lag)).astype(BF16)
    both = dot(fwd_ref[:, :half], bank, (((1,), (1,)), ((), ())))
    spectrum = both[:WIN] + both[WIN:]
    h_re, h_im = spectrum[:half], spectrum[half:]
    first = lax.broadcasted_iota(jnp.int32, h_re.shape, 0) == 0
    h_last = jnp.where(first, h_im, h_re)
    h_im = jnp.where(first, 0.0, h_im)

    prod[:TAPS] = halo_ref[:TAPS]
    raw = halo_ref[TAPS:].astype(F32)[:8]
    for b in range(TOK // TAPS):
        made = []
        for s in range(3):
            taps = [taps_ref[j, s : s + 1, :] for j in range(3)]
            if b:
                rows = x_ref[s, b * TAPS - 16 : (b + 1) * TAPS, :].astype(F32)
            else:
                rows = jnp.concatenate([rolled(raw, 6 - 2 * s), x_ref[s, :TAPS, :].astype(F32)], axis=0)
            made.append(featurize(rows, taps, TAPS))
        query[b * TAPS : (b + 1) * TAPS] = made[0]
        prod[(b + 1) * TAPS : (b + 2) * TAPS] = (made[1].astype(F32) * made[2].astype(F32)).astype(BF16)

    for b in range(TOK // TAPS):
        both = dot(fwd_ref[...], prod[b * TAPS : b * TAPS + WIN], plain)
        spectrum = both[:WIN] + both[WIN:]
        re, im = spectrum[:half], spectrum[half:]
        y = jnp.concatenate([re * h_re - im * h_im, re * h_im + im * h_last], axis=0)
        high = y.astype(BF16)
        low = (y - high.astype(F32)).astype(BF16)
        long_part = dot(inv_ref[...], jnp.concatenate([high, low, high], axis=0), plain)
        here = prod[(b + 1) * TAPS : (b + 2) * TAPS].astype(F32)
        q = query[b * TAPS : (b + 1) * TAPS].astype(F32)
        out_ref[b * TAPS : (b + 1) * TAPS, :] = (q * (long_part + gain_ref[...] * here)).astype(BF16)


def mixer(x, halo, taps, filt, rate, gain):
    forward, inverse = transform_matrices()
    steps = CH // LANES
    return pl.pallas_call(
        mixer_kernel,
        grid=(steps,),
        in_specs=[
            pl.BlockSpec((3, TOK, LANES), lambda i: (0, 0, i)),
            pl.BlockSpec((TAPS + 16, LANES), lambda i: (0, i)),
            pl.BlockSpec((3, 3, LANES), lambda i: (0, 0, i)),
            pl.BlockSpec((LANES, TAPS), lambda i: (i, 0)),
            pl.BlockSpec((LANES, 1), lambda i: (i, 0)),
            pl.BlockSpec((1, LANES), lambda i: (0, i)),
            pl.BlockSpec(forward.shape, lambda i: (0, 0)),
            pl.BlockSpec(inverse.shape, lambda i: (0, 0)),
        ],
        out_specs=pl.BlockSpec((TOK, LANES), lambda i: (0, i)),
        out_shape=jax.ShapeDtypeStruct((TOK, CH), BF16),
        scratch_shapes=[
            pltpu.VMEM((TOK + TAPS, LANES), BF16),
            pltpu.VMEM((TOK, LANES), BF16),
        ],
        compiler_params=pltpu.CompilerParams(vmem_limit_bytes=32 << 20),
        cost_estimate=pl.CostEstimate(flops=2 * 900 * 10**6, bytes_accessed=6 << 20, transcendentals=CH * TAPS),
    )(x, halo, taps, filt, rate[:, None], gain[None, :], jnp.asarray(forward), jnp.asarray(inverse))


def project_kernel(where_ref, acts_ref, *refs):
    n_src = len(PIECES)
    src, (out_ref, acts, weight, act_sems, w_sems) = refs[:n_src], refs[n_src:]
    y, z = where_ref[0], where_ref[1]
    for k in range(8):
        pltpu.make_async_copy(acts_ref.at[k], acts.at[k], act_sems.at[k]).start()
    pending = [[] for _ in range(4)]
    n = 0
    for ref, (kind, j_list, i_list) in zip(src, PIECES, strict=True):
        for a, j in enumerate(j_list):
            for e, i in enumerate(i_list):
                view = ref.at[e] if kind == "A" else ref.at[a]
                row = 0 if kind == "A" else CH // 2
                target = weight.at[i // 2, j, pl.ds(row, CH // 2), pl.ds((i % 2) * 128, 128)]
                pending[i // 2].append((n, view, target))
                n += 1
    copies = []
    for p in range(4):
        group = [pltpu.make_async_copy(view, target, w_sems.at[n]) for n, view, target in pending[p]]
        for copy in group:
            copy.start()
        copies.append(group)
    for k in range(8):
        pltpu.make_async_copy(acts_ref.at[k], acts.at[k], act_sems.at[k]).wait()
    for p in range(4):
        for copy in copies[p]:
            copy.wait()

        def rows_step(m, carry):
            start = pl.multiple_of((m % 2) * 256, 256)
            total = None
            for j in range(4):
                block = (m // 2) * 4 + lax.rem(y + j, 4)
                term = jnp.dot(acts[block, pl.ds(start, 256), :], weight[p, j], preferred_element_type=F32)
                total = term if total is None else total + term
            rounded = total.astype(BF16)
            row = pl.multiple_of(m * 256, 256)
            for e in range(2):
                col = pl.multiple_of(lax.rem(z + 2 * p + e, 8) * 128, 128)
                out_ref[pl.ds(row, 256), pl.ds(col, 128)] = rounded[:, e * 128 : (e + 1) * 128]
            return carry

        lax.fori_loop(0, 4, rows_step, 0)


PIECES = (
    [("A", [0], list(range(8))), ("A", [1], list(range(8))), ("A", [3], list(range(8)))]
    + [("A", [2], [0, 1, 2, 3]), ("A", [2], [4, 5, 6, 7])]
    + [("B", [0, 1, 2, 3], [i]) for i in (0, 1, 2, 3, 5, 6, 7)]
    + [("B", [0, 1], [4]), ("B", [2, 3], [4])]
)


def project(where, acts, pieces):
    any_space = pl.BlockSpec(memory_space=pl.ANY)
    n_copies = sum(len(j) * len(i) for _, j, i in PIECES)
    return pl.pallas_call(
        project_kernel,
        in_specs=[pl.BlockSpec(memory_space=pltpu.SMEM)] + [any_space] * (1 + len(pieces)),
        out_specs=pl.BlockSpec(memory_space=pltpu.VMEM),
        out_shape=jax.ShapeDtypeStruct((2 * TOK, CH), BF16),
        scratch_shapes=[
            pltpu.VMEM((8, TOK, CH), BF16),
            pltpu.VMEM((4, 4, CH, 256), BF16),
            pltpu.SemaphoreType.DMA((8,)),
            pltpu.SemaphoreType.DMA((n_copies,)),
        ],
        compiler_params=pltpu.CompilerParams(vmem_limit_bytes=48 << 20),
        cost_estimate=pl.CostEstimate(flops=2 * 1024 * 4096 * 1024, bytes_accessed=20 << 20, transcendentals=0),
    )(where, acts, *pieces)


def shift(value, axis, steps):
    size = lax.axis_size(axis)
    return lax.ppermute(value, axis, [(i, (i + steps) % size) for i in range(size)])


def gather_weight(own):
    a0, b0 = own[: CH // 2], own[CH // 2 :]
    a = {0: a0}
    for d in (1, 2, 3):
        a[d] = shift(a[d - 1], "z", -1)
        a[8 - d] = shift(a[(9 - d) % 8], "z", 1)
    a[4] = jnp.concatenate([shift(a[3][: CH // 4], "z", -1), shift(a[5][CH // 4 :], "z", 1)])
    b = {0: b0, 1: shift(b0, "y", -1), 3: shift(b0, "y", 1)}
    b[2] = jnp.concatenate([shift(b[1][: CH // 4], "y", -1), shift(b[3][CH // 4 :], "y", 1)])
    big_a = jnp.stack([a[i] for i in range(8)])
    big_b = jnp.stack([b[j] for j in range(4)])
    a1, a3 = shift(big_a, "y", -1), shift(big_a, "y", 1)
    a2_low, a2_high = shift(a1[:4], "y", -1), shift(a3[4:], "y", 1)
    up, down = {0: big_b}, {0: big_b}
    for d in (1, 2, 3):
        up[d] = shift(up[d - 1], "z", -1)
        down[d] = shift(down[d - 1], "z", 1)
    b4_low, b4_high = shift(up[3][:2], "z", -1), shift(down[3][2:], "z", 1)
    return [big_a, a1, a3, a2_low, a2_high, big_b, up[1], up[2], up[3], down[3], down[2], down[1], b4_low, b4_high]


def on_device(projected, short_taps, filter_taps, decay_rates, bypass_gain, out_weight):
    swap = [(y * 4 + t, t * 4 + y) for y in range(4) for t in range(4)]
    own = lax.ppermute(out_weight, ("y", "xl", "c"), swap)
    x = jnp.transpose(projected, (1, 0, 2))
    tail = tail_rows(x, short_taps)
    halo = lax.ppermute(tail, ("y", "xh", "z"), [(i, i + 1) for i in range(63)])
    gated = mixer(x, halo, short_taps, filter_taps, decay_rates, bypass_gain)
    acts = lax.all_gather(gated, CELL, axis=0, tiled=False)
    pieces = gather_weight(own)
    where = jnp.stack([lax.axis_index("y"), lax.axis_index("z")]).astype(jnp.int32)
    mine = project(where, acts, pieces)
    got = lax.all_to_all(mine.reshape(8, TOK // 4, CH), CELL, 0, 0, tiled=True)
    got = got.reshape(2, 4, TOK // 4, CH)
    return jnp.transpose(got, (2, 1, 0, 3)).reshape(TOK // 4, 8 * CH)


def solution(mesh):
    fine = Mesh(mesh.devices.reshape(4, 2, 8, 2, 2), ("y", "xh", "z", "xl", "c"))
    ctx, tp = ("y", "xh", "z"), ("xl", "c")
    return jax.shard_map(
        on_device,
        mesh=fine,
        in_specs=(P(ctx, None, tp), P(None, None, tp), P(tp, None), P(tp), P(tp), P(tp, ctx)),
        out_specs=P(ctx + tp, None),
        check_vma=False,
    )
```

```python
import functools

import jax
import jax.numpy as jnp
import ml_dtypes
import numpy as np
from jax import lax
from jax.experimental import pallas as pl
from jax.experimental.pallas import tpu as pltpu
from jax.sharding import Mesh
from jax.sharding import PartitionSpec as P

TOK = 512
CH = 1024
TAPS = 128
WIN = 256
LANES = 256
CHUNKS = ((0, 1, 7, 2, 6), (3, 5, 4))
VMEM = 56 << 20
F32, BF16 = jnp.float32, jnp.bfloat16


def two_halves(matrix):
    high = matrix.astype(ml_dtypes.bfloat16)
    low = (matrix - high.astype(np.float64)).astype(ml_dtypes.bfloat16)
    return high, low


@functools.lru_cache(maxsize=None)
def transform_matrices():
    at = np.arange(WIN)
    half = WIN // 2
    angle = 2 * np.pi * (np.outer(np.arange(half), at) % WIN) / WIN
    sine = -np.sin(angle)
    sine[0] = np.cos(np.pi * at)
    forward = np.concatenate([np.cos(angle), sine])
    scale = np.where(np.arange(half) == 0, 1.0, 2.0)[:, None] / WIN
    scale_im = np.where(np.arange(half) == 0, 1.0, 2.0)[:, None] / WIN
    inverse = np.concatenate([np.cos(angle) * scale, sine * scale_im]).T[half:]
    fh, fl = two_halves(forward)
    ih, il = two_halves(inverse)
    return np.concatenate([fh, fl]), np.concatenate([ih, ih, il], axis=1)


def rolled(x, steps):
    return pltpu.roll(x, steps % x.shape[0], 0)


def featurize(rows, taps, count):
    lead = rows.shape[0] - count
    one = rolled(rows, 1)[lead:]
    two = rolled(rows, 2)[lead:]
    return (taps[0] * rows[lead:] + taps[1] * one + taps[2] * two).astype(BF16)


def tail_kernel(x_ref, before_ref, taps_ref, out_ref):
    streams = []
    raw = []
    for s in range(3):
        rows = x_ref[s].astype(F32)
        raw.append(rows[-8:])
        if s:
            taps = [taps_ref[j, s : s + 1, :] for j in range(3)]
            rows = jnp.concatenate([before_ref[s].astype(F32), rows], axis=0)
            streams.append(featurize(rows, taps, TAPS).astype(F32))
    out_ref[:TAPS, :] = (streams[0] * streams[1]).astype(BF16)
    row = lax.broadcasted_iota(jnp.int32, raw[0].shape, 0)
    packed = jnp.where(row < 2, rolled(raw[0], 2), jnp.where(row < 4, rolled(raw[1], 4), rolled(raw[2], 6)))
    out_ref[TAPS:, :] = jnp.concatenate([packed, jnp.zeros_like(packed)], axis=0).astype(BF16)


def tail_rows(x, taps):
    width = CH // 2
    return pl.pallas_call(
        tail_kernel,
        grid=(CH // width,),
        in_specs=[
            pl.BlockSpec((3, TAPS, width), lambda i: (0, TOK // TAPS - 1, i)),
            pl.BlockSpec((3, 16, width), lambda i: (0, (TOK - TAPS) // 16 - 1, i)),
            pl.BlockSpec((3, 3, width), lambda i: (0, 0, i)),
        ],
        out_specs=pl.BlockSpec((TAPS + 16, width), lambda i: (0, i)),
        out_shape=jax.ShapeDtypeStruct((TAPS + 16, CH), BF16),
        compiler_params=pltpu.CompilerParams(vmem_limit_bytes=VMEM),
        cost_estimate=pl.CostEstimate(flops=4 * TAPS * CH, bytes_accessed=2 << 20, transcendentals=0),
    )(x, x, taps)


def mixer_kernel(x_ref, halo_ref, taps_ref, filt_ref, rate_ref, gain_ref, fwd_ref, inv_ref, out_ref, prod, query):
    dot = functools.partial(lax.dot_general, preferred_element_type=F32)
    plain = (((1,), (0,)), ((), ()))
    half = WIN // 2

    lag = lax.broadcasted_iota(jnp.int32, (TAPS, LANES), 0).astype(F32)
    bank = (filt_ref[...].T * jnp.exp(-rate_ref[...] * lag)).astype(BF16)
    both = dot(fwd_ref[:, :half], bank, plain)
    spectrum = both[:WIN] + both[WIN:]
    h_re, h_im = spectrum[:half], spectrum[half:]
    first = lax.broadcasted_iota(jnp.int32, h_re.shape, 0) == 0
    h_last = jnp.where(first, h_im, h_re)
    h_im = jnp.where(first, 0.0, h_im)

    prod[:TAPS] = halo_ref[:TAPS]
    raw = halo_ref[TAPS:].astype(F32)[:8]
    for b in range(TOK // TAPS):
        made = []
        for s in range(3):
            taps = [taps_ref[j, s : s + 1, :] for j in range(3)]
            if b:
                rows = x_ref[s, b * TAPS - 16 : (b + 1) * TAPS, :].astype(F32)
            else:
                rows = jnp.concatenate([rolled(raw, 6 - 2 * s), x_ref[s, :TAPS, :].astype(F32)], axis=0)
            made.append(featurize(rows, taps, TAPS))
        query[b * TAPS : (b + 1) * TAPS] = made[0]
        prod[(b + 1) * TAPS : (b + 2) * TAPS] = (made[1].astype(F32) * made[2].astype(F32)).astype(BF16)

    for b in range(TOK // TAPS):
        both = dot(fwd_ref[...], prod[b * TAPS : b * TAPS + WIN], plain)
        spectrum = both[:WIN] + both[WIN:]
        re, im = spectrum[:half], spectrum[half:]
        y = jnp.concatenate([re * h_re - im * h_im, re * h_im + im * h_last], axis=0)
        high = y.astype(BF16)
        low = (y - high.astype(F32)).astype(BF16)
        long_part = dot(inv_ref[...], jnp.concatenate([high, low, high], axis=0), plain)
        here = prod[(b + 1) * TAPS : (b + 2) * TAPS].astype(F32)
        q = query[b * TAPS : (b + 1) * TAPS].astype(F32)
        out_ref[b * TAPS : (b + 1) * TAPS, :] = (q * (long_part + gain_ref[...] * here)).astype(BF16)


def mixer(x, halo, taps, filt, rate, gain):
    forward, inverse = transform_matrices()
    steps = CH // LANES
    return pl.pallas_call(
        mixer_kernel,
        grid=(steps,),
        in_specs=[
            pl.BlockSpec((3, TOK, LANES), lambda i: (0, 0, i)),
            pl.BlockSpec((TAPS + 16, LANES), lambda i: (0, i)),
            pl.BlockSpec((3, 3, LANES), lambda i: (0, 0, i)),
            pl.BlockSpec((LANES, TAPS), lambda i: (i, 0)),
            pl.BlockSpec((1, LANES), lambda i: (0, i)),
            pl.BlockSpec((1, LANES), lambda i: (0, i)),
            pl.BlockSpec(forward.shape, lambda i: (0, 0)),
            pl.BlockSpec(inverse.shape, lambda i: (0, 0)),
        ],
        out_specs=pl.BlockSpec((TOK, LANES), lambda i: (0, i)),
        out_shape=jax.ShapeDtypeStruct((TOK, CH), BF16),
        scratch_shapes=[
            pltpu.VMEM((TOK + TAPS, LANES), BF16),
            pltpu.VMEM((TOK, LANES), BF16),
        ],
        compiler_params=pltpu.CompilerParams(vmem_limit_bytes=VMEM),
        cost_estimate=pl.CostEstimate(flops=2 * 900 * 10**6, bytes_accessed=6 << 20, transcendentals=CH * TAPS),
    )(x, halo, taps, filt, rate[None, :], gain[None, :], jnp.asarray(forward), jnp.asarray(inverse))


def k_block(y, kind):
    if kind > 1:
        y = lax.rem(y + (1 if kind == 2 else 3), 4)
    return lax.rem(y, 2) * 2 + (1 - y // 2 if kind == 1 else y // 2)


def project_kernel(n_pieces, moves, absolute, pinned, where_ref, *refs):
    n_acts = 1 if pinned else 8
    act_refs, src, rest = refs[:n_acts], refs[n_acts : n_acts + n_pieces], refs[n_acts + n_pieces :]
    n_out = 1 if absolute else 4
    outs, rest = rest[:n_out], rest[n_out:]
    if pinned:
        weight, result, sems = rest
        acts = act_refs[0]
    else:
        acts, weight, result, sems, act_sems = rest
    y, x, c = where_ref[0], where_ref[2], where_ref[3]
    act_copies = []
    for k in range(0 if pinned else 8):
        core = c if k < 4 else 1 - c
        chip = lax.rem(x + 4 + (0, 2 * core - 1, 1 - 2 * core, 2)[k % 4], 4)
        block = lax.rem(chip, 2) * 2 + core
        view = act_refs[k]
        target = acts.at[chip // 2, :, pl.ds(pl.multiple_of(block * CH, CH), CH)]
        act_copies.append(pltpu.make_async_copy(view, target, act_sems.at[chip // 2, block]))
    copies = []
    for n, (piece, row, col, kind) in enumerate(moves):
        start = pl.multiple_of(k_block(y, kind) * CH, CH)
        target = weight.at[pl.ds(start, CH), pl.ds(col * 128, 128)]
        copies.append(pltpu.make_async_copy(src[piece].at[pl.ds(row, CH)], target, sems.at[n]))
    for copy in act_copies[:1] + act_copies[4:5] + copies + act_copies[1:4] + act_copies[5:]:
        copy.start()
    for copy in copies:
        copy.wait()
    columns = weight.shape[1]
    for turn in range(2):
        half = x // 2 if turn == 0 else 1 - x // 2
        for block in range(0 if pinned else 4):
            view = acts.at[half, :, pl.ds(block * CH, CH)]
            pltpu.make_async_copy(act_refs[0], view, act_sems.at[half, block]).wait()
        rows = pl.ds(pl.multiple_of(half * TOK, TOK), TOK)
        for at in range(0, columns, 256):
            span = slice(at, min(at + 256, columns))
            result[rows, span] = jnp.dot(acts[half], weight[:, span], preferred_element_type=F32).astype(BF16)
    if absolute:
        for device in range(8):
            outs[0][device] = result[device * 128 : (device + 1) * 128]
    else:
        for step in range(4):
            for other in range(2):
                core = c if other == 0 else 1 - c
                row = pl.multiple_of((lax.rem(x + step, 4) * 2 + core) * 128, 128)
                outs[step][other] = result[pl.ds(row, 128), :]


def project(where, acts, pieces, moves, columns, absolute):
    any_space, vmem = pl.BlockSpec(memory_space=pl.ANY), pl.BlockSpec(memory_space=pltpu.VMEM)
    width = columns * 128
    if absolute:
        shapes = [jax.ShapeDtypeStruct((8, 128, width), BF16)]
    else:
        shapes = [jax.ShapeDtypeStruct((2, 128, width), BF16)] * 4
    scratch = [
        pltpu.VMEM((4 * CH, width), BF16),
        pltpu.VMEM((2 * TOK, width), BF16),
        pltpu.SemaphoreType.DMA((len(moves),)),
    ]
    pinned = len(acts) == 1
    if pinned:
        acts = [pltpu.with_memory_space_constraint(acts[0], pltpu.VMEM)]
    else:
        shapes = shapes + [pltpu.VMEM((2, TOK, 4 * CH), BF16)]
        scratch.append(pltpu.SemaphoreType.DMA((2, 4)))
    act_specs = [vmem] if pinned else [any_space] * 8
    return pl.pallas_call(
        functools.partial(project_kernel, len(pieces), moves, absolute, pinned),
        in_specs=[pl.BlockSpec(memory_space=pltpu.SMEM)] + act_specs + [any_space] * len(pieces),
        out_specs=[vmem] * len(shapes),
        out_shape=shapes,
        scratch_shapes=scratch,
        compiler_params=pltpu.CompilerParams(vmem_limit_bytes=(40 if pinned else 52) << 20),
        cost_estimate=pl.CostEstimate(flops=2 * 1024 * 4096 * width, bytes_accessed=12 << 20, transcendentals=0),
    )(where, *acts, *pieces)


def assemble_kernel(where_ref, *refs):
    out_ref = refs[-1]
    z, x, c = where_ref[1], where_ref[2], where_ref[3]

    def put(chip, core, columns, value):
        base = ((lax.rem(chip, 2) * 2 + core) * 2 + chip // 2) * 8
        for e, i in enumerate(columns):
            col = pl.multiple_of((base + lax.rem(z + i, 8)) * 128, 128)
            out_ref[:, pl.ds(col, 128)] = value[:, e * 128 : (e + 1) * 128]

    for chunk, columns in enumerate(CHUNKS[:-1]):
        parts = refs[chunk * 5 : chunk * 5 + 5]
        for step in range(4):
            chip = lax.rem(x + 4 - step, 4)
            put(chip, c, columns, parts[step][0])
            put(chip, 1 - c, columns, parts[4][step])
    for device in range(8):
        put(jnp.int32(device // 2), device % 2, CHUNKS[-1], refs[-2][device])


def assemble(where, parts):
    vmem = pl.BlockSpec(memory_space=pltpu.VMEM)
    return pl.pallas_call(
        assemble_kernel,
        in_specs=[pl.BlockSpec(memory_space=pltpu.SMEM)] + [vmem] * len(parts),
        out_specs=vmem,
        out_shape=jax.ShapeDtypeStruct((TOK // 4, 8 * CH), BF16),
        compiler_params=pltpu.CompilerParams(vmem_limit_bytes=24 << 20),
        cost_estimate=pl.CostEstimate(flops=0, bytes_accessed=4 << 20, transcendentals=0),
    )(where, *parts)


def shift(value, axis, steps):
    size = lax.axis_size(axis)
    return lax.ppermute(value, axis, [(i, (i + steps) % size) for i in range(size)])


def opposite(value, axis, size, first):
    pairs = [(2 * i + c, 2 * ((i + (first if c == 0 else -first)) % size) + c) for i in range(size) for c in range(2)]
    return lax.ppermute(value, (axis, "c") if isinstance(axis, str) else axis + ("c",), pairs)


def exchange(value, kind):
    held = [(d % 2) * 2 + (1 - d // 2 if kind else d // 2) for d in range(4)]
    pairs = [(a * 4 + b, held.index(b) * 4 + a) for a in range(4) for b in range(4)]
    return lax.ppermute(value, ("y", "xl", "c"), pairs)


def swap_cores(value):
    return lax.ppermute(value, "c", [(0, 1), (1, 0)])


def together(*values):
    return lax.optimization_barrier(values)


RING = ("xh", "xl")


def on_device(projected, short_taps, filter_taps, decay_rates, bypass_gain, out_weight):
    chip = lax.axis_index("xh") * 2 + lax.axis_index("xl")
    where = jnp.stack([lax.axis_index("y"), lax.axis_index("z"), chip, lax.axis_index("c")]).astype(jnp.int32)

    places = {i: [] for i in range(8)}
    buffers = []
    column = {}

    def keep_column(i, buffer):
        column[i] = buffer
        places[i] += [(len(buffers), 0, 0), (len(buffers), CH, 1)]
        buffers.append(buffer)

    def along_y(*columns):
        rows = [column[i][:CH] for i in columns]
        rows = rows[0] if len(rows) == 1 else jnp.concatenate(rows)
        return shift(rows, "y", -1), shift(rows, "y", 1)

    def keep_rows(columns, *both):
        for kind, buffer in zip((2, 3), both, strict=True):
            for e, i in enumerate(columns):
                places[i].append((len(buffers), e * CH, kind))
            buffers.append(buffer)

    def work_on(columns, acts, absolute):
        used, moves = [], []
        for col, i in enumerate(columns):
            for n, row, kind in places[i]:
                if n not in used:
                    used.append(n)
                moves.append((used.index(n), row, col, kind))
        return project(where, acts, [buffers[n] for n in used], tuple(moves), len(columns), absolute)

    def to_cell(sent):
        return [shift(sent[step], RING, step) for step in (1, 2, 3)]

    def other_cores(got):
        return swap_cores(jnp.stack([g[1] for g in got]))

    x = jnp.transpose(projected, (1, 0, 2))
    tail = tail_rows(x, short_taps)
    halo = lax.ppermute(tail, ("y", "xh", "z"), [(i, i + 1) for i in range(63)])
    blocks = [exchange(out_weight, 0), exchange(out_weight, 1)]
    gated = mixer(x, halo, short_taps, filter_taps, decay_rates, bypass_gain)
    *blocks, gated = together(*blocks, gated)
    keep_column(0, jnp.concatenate(blocks))
    one = opposite(gated, RING, 4, 1)
    first, last, *rows, one = together(shift(column[0], "z", -1), shift(column[0], "z", 1), *along_y(0), one)
    keep_column(1, first)
    keep_column(7, last)
    keep_rows((0,), *rows)
    two = opposite(together(gated, first)[0], RING, 4, -1)
    first, last, *rows, two = together(shift(column[1], "z", -1), shift(column[7], "z", 1), *along_y(1, 7), two)
    keep_column(2, first)
    keep_column(6, last)
    keep_rows((1, 7), *rows)
    three = opposite(together(one, first)[0], RING, 4, 1)
    first, last, *rows, three = together(shift(column[2], "z", -1), shift(column[6], "z", 1), *along_y(2, 6), three)
    keep_column(3, first)
    keep_column(5, last)
    keep_rows((2, 6), *rows)
    own, one, two, three, _ = together(gated, one, two, three, first)
    acts = [own, one, two, three] + [swap_cores(v) for v in (own, one, two, three)]
    *sent, held = work_on(CHUNKS[0], acts, False)
    middle, *rows = together(shift(column[3], "z", -1), *along_y(3, 5), *sent)
    rows, sent = rows[:2], rows[2:]
    keep_column(4, middle)
    keep_rows((3, 5), *rows)
    own_0, got_0 = sent[0], to_cell(sent)
    rows = together(*along_y(4))
    keep_rows((4,), *rows)
    (last_sent,) = work_on(CHUNKS[1], [held], True)
    *got_0, last_sent = together(*got_0, last_sent)
    swapped_0 = other_cores([own_0] + got_0)
    last_got = lax.all_to_all(last_sent, RING + ("c",), 0, 0, tiled=True)
    return assemble(where, [own_0, *got_0, swapped_0, last_got])


def solution(mesh):
    fine = Mesh(mesh.devices.reshape(4, 2, 8, 2, 2), ("y", "xh", "z", "xl", "c"))
    ctx, tp = ("y", "xh", "z"), ("xl", "c")
    return jax.shard_map(
        on_device,
        mesh=fine,
        in_specs=(P(ctx, None, tp), P(None, None, tp), P(tp, None), P(tp), P(tp), P(tp, ctx)),
        out_specs=P(ctx + tp, None),
        check_vma=False,
    )
```

```python
import functools

import jax
import jax.numpy as jnp
import ml_dtypes
import numpy as np
from jax import lax
from jax.experimental import pallas as pl
from jax.experimental.pallas import tpu as pltpu
from jax.sharding import Mesh
from jax.sharding import PartitionSpec as P

TOK = 512
CH = 1024
TAPS = 128
WIN = 256
LANES = 256
CHUNKS = ((0, 1, 7, 2, 6), (3, 5, 4))
VMEM = 56 << 20
F32, BF16 = jnp.float32, jnp.bfloat16


def two_halves(matrix):
    high = matrix.astype(ml_dtypes.bfloat16)
    low = (matrix - high.astype(np.float64)).astype(ml_dtypes.bfloat16)
    return high, low


@functools.lru_cache(maxsize=None)
def transform_matrices():
    at = np.arange(WIN)
    half = WIN // 2
    angle = 2 * np.pi * (np.outer(np.arange(half), at) % WIN) / WIN
    sine = -np.sin(angle)
    sine[0] = np.cos(np.pi * at)
    forward = np.concatenate([np.cos(angle), sine])
    scale = np.where(np.arange(half) == 0, 1.0, 2.0)[:, None] / WIN
    scale_im = np.where(np.arange(half) == 0, 1.0, 2.0)[:, None] / WIN
    inverse = np.concatenate([np.cos(angle) * scale, sine * scale_im]).T[half:]
    fh, fl = two_halves(forward)
    ih, il = two_halves(inverse)
    return np.concatenate([fh, fl]), np.concatenate([ih, ih, il], axis=1)


def rolled(x, steps):
    return pltpu.roll(x, steps % x.shape[0], 0)


def featurize(rows, taps, count):
    lead = rows.shape[0] - count
    one = rolled(rows, 1)[lead:]
    two = rolled(rows, 2)[lead:]
    return (taps[0] * rows[lead:] + taps[1] * one + taps[2] * two).astype(BF16)


def tail_kernel(x_ref, before_ref, taps_ref, out_ref):
    streams = []
    raw = []
    for s in range(3):
        rows = x_ref[s].astype(F32)
        raw.append(rows[-8:])
        if s:
            taps = [taps_ref[j, s : s + 1, :] for j in range(3)]
            rows = jnp.concatenate([before_ref[s].astype(F32), rows], axis=0)
            streams.append(featurize(rows, taps, TAPS).astype(F32))
    out_ref[:TAPS, :] = (streams[0] * streams[1]).astype(BF16)
    row = lax.broadcasted_iota(jnp.int32, raw[0].shape, 0)
    packed = jnp.where(row < 2, rolled(raw[0], 2), jnp.where(row < 4, rolled(raw[1], 4), rolled(raw[2], 6)))
    out_ref[TAPS:, :] = jnp.concatenate([packed, jnp.zeros_like(packed)], axis=0).astype(BF16)


def tail_rows(x, taps):
    width = CH // 2
    return pl.pallas_call(
        tail_kernel,
        grid=(CH // width,),
        in_specs=[
            pl.BlockSpec((3, TAPS, width), lambda i: (0, TOK // TAPS - 1, i)),
            pl.BlockSpec((3, 16, width), lambda i: (0, (TOK - TAPS) // 16 - 1, i)),
            pl.BlockSpec((3, 3, width), lambda i: (0, 0, i)),
        ],
        out_specs=pl.BlockSpec((TAPS + 16, width), lambda i: (0, i)),
        out_shape=jax.ShapeDtypeStruct((TAPS + 16, CH), BF16),
        compiler_params=pltpu.CompilerParams(vmem_limit_bytes=VMEM),
        cost_estimate=pl.CostEstimate(flops=4 * TAPS * CH, bytes_accessed=2 << 20, transcendentals=0),
    )(x, x, taps)


def mixer_kernel(x_ref, halo_ref, taps_ref, filt_ref, rate_ref, gain_ref, fwd_ref, inv_ref, out_ref, prod, query):
    dot = functools.partial(lax.dot_general, preferred_element_type=F32)
    plain = (((1,), (0,)), ((), ()))
    half = WIN // 2

    lag = lax.broadcasted_iota(jnp.int32, (TAPS, LANES), 0).astype(F32)
    bank = (filt_ref[...].T * jnp.exp(-rate_ref[...] * lag)).astype(BF16)
    both = dot(fwd_ref[:, :half], bank, plain)
    spectrum = both[:WIN] + both[WIN:]
    h_re, h_im = spectrum[:half], spectrum[half:]
    first = lax.broadcasted_iota(jnp.int32, h_re.shape, 0) == 0
    h_last = jnp.where(first, h_im, h_re)
    h_im = jnp.where(first, 0.0, h_im)

    prod[:TAPS] = halo_ref[:TAPS]
    raw = halo_ref[TAPS:].astype(F32)[:8]
    for b in range(TOK // TAPS):
        made = []
        for s in range(3):
            taps = [taps_ref[j, s : s + 1, :] for j in range(3)]
            if b:
                rows = x_ref[s, b * TAPS - 16 : (b + 1) * TAPS, :].astype(F32)
            else:
                rows = jnp.concatenate([rolled(raw, 6 - 2 * s), x_ref[s, :TAPS, :].astype(F32)], axis=0)
            made.append(featurize(rows, taps, TAPS))
        query[b * TAPS : (b + 1) * TAPS] = made[0]
        prod[(b + 1) * TAPS : (b + 2) * TAPS] = (made[1].astype(F32) * made[2].astype(F32)).astype(BF16)

    for b in range(TOK // TAPS):
        both = dot(fwd_ref[...], prod[b * TAPS : b * TAPS + WIN], plain)
        spectrum = both[:WIN] + both[WIN:]
        re, im = spectrum[:half], spectrum[half:]
        y = jnp.concatenate([re * h_re - im * h_im, re * h_im + im * h_last], axis=0)
        high = y.astype(BF16)
        low = (y - high.astype(F32)).astype(BF16)
        long_part = dot(inv_ref[...], jnp.concatenate([high, low, high], axis=0), plain)
        here = prod[(b + 1) * TAPS : (b + 2) * TAPS].astype(F32)
        q = query[b * TAPS : (b + 1) * TAPS].astype(F32)
        out_ref[b * TAPS : (b + 1) * TAPS, :] = (q * (long_part + gain_ref[...] * here)).astype(BF16)


def mixer(x, halo, taps, filt, rate, gain):
    forward, inverse = transform_matrices()
    steps = CH // LANES
    return pl.pallas_call(
        mixer_kernel,
        grid=(steps,),
        in_specs=[
            pl.BlockSpec((3, TOK, LANES), lambda i: (0, 0, i)),
            pl.BlockSpec((TAPS + 16, LANES), lambda i: (0, i)),
            pl.BlockSpec((3, 3, LANES), lambda i: (0, 0, i)),
            pl.BlockSpec((LANES, TAPS), lambda i: (i, 0)),
            pl.BlockSpec((1, LANES), lambda i: (0, i)),
            pl.BlockSpec((1, LANES), lambda i: (0, i)),
            pl.BlockSpec(forward.shape, lambda i: (0, 0)),
            pl.BlockSpec(inverse.shape, lambda i: (0, 0)),
        ],
        out_specs=pl.BlockSpec((TOK, LANES), lambda i: (0, i)),
        out_shape=jax.ShapeDtypeStruct((TOK, CH), BF16),
        scratch_shapes=[
            pltpu.VMEM((TOK + TAPS, LANES), BF16),
            pltpu.VMEM((TOK, LANES), BF16),
        ],
        compiler_params=pltpu.CompilerParams(vmem_limit_bytes=VMEM),
        cost_estimate=pl.CostEstimate(flops=2 * 900 * 10**6, bytes_accessed=6 << 20, transcendentals=CH * TAPS),
    )(x, halo, taps, filt, rate[None, :], gain[None, :], jnp.asarray(forward), jnp.asarray(inverse))


def k_block(y, kind):
    if kind > 1:
        y = lax.rem(y + (1 if kind == 2 else 3), 4)
    return lax.rem(y, 2) * 2 + (1 - y // 2 if kind == 1 else y // 2)


def project_kernel(n_pieces, moves, absolute, pinned, n_before, where_ref, *refs):
    n_acts = 1 if pinned else 8
    act_refs, src, rest = refs[:n_acts], refs[n_acts : n_acts + n_pieces], refs[n_acts + n_pieces :]
    before, rest = rest[:n_before], rest[n_before:]
    n_out = 1 if absolute else 4
    outs, rest = rest[:n_out], rest[n_out:]
    if pinned:
        weight, result, sems = rest
        acts = act_refs[0]
    else:
        acts, weight, result, sems, act_sems = rest
    y, x, c = where_ref[0], where_ref[2], where_ref[3]
    act_copies = []
    for k in range(0 if pinned else 8):
        core = c if k < 4 else 1 - c
        chip = lax.rem(x + 4 + (0, 2 * core - 1, 1 - 2 * core, 2)[k % 4], 4)
        block = lax.rem(chip, 2) * 2 + core
        view = act_refs[k]
        target = acts.at[chip // 2, :, pl.ds(pl.multiple_of(block * CH, CH), CH)]
        act_copies.append(pltpu.make_async_copy(view, target, act_sems.at[chip // 2, block]))
    copies = []
    for n, (piece, row, col, kind) in enumerate(moves):
        start = pl.multiple_of(k_block(y, kind) * CH, CH)
        target = weight.at[pl.ds(start, CH), pl.ds(col * 128, 128)]
        copies.append(pltpu.make_async_copy(src[piece].at[pl.ds(row, CH)], target, sems.at[n]))
    for copy in act_copies[:1] + act_copies[4:5] + copies + act_copies[1:4] + act_copies[5:]:
        copy.start()
    for copy in copies:
        copy.wait()
    columns = weight.shape[1]
    for turn in range(2):
        half = x // 2 if turn == 0 else 1 - x // 2
        for block in range(0 if pinned else 4):
            view = acts.at[half, :, pl.ds(block * CH, CH)]
            pltpu.make_async_copy(act_refs[0], view, act_sems.at[half, block]).wait()
        rows = pl.ds(pl.multiple_of(half * TOK, TOK), TOK)
        for at in range(0, columns, 256):
            span = slice(at, min(at + 256, columns))
            result[rows, span] = jnp.dot(acts[half], weight[:, span], preferred_element_type=F32).astype(BF16)
    if absolute:
        kept = 0
        for ref in before:
            outs[0][:, :, : ref.shape[2]] = ref[...]
            kept = ref.shape[2]
        for device in range(8):
            outs[0][device, :, kept:] = result[device * 128 : (device + 1) * 128]
    else:
        for step in range(4):
            for other in range(2):
                core = c if other == 0 else 1 - c
                row = pl.multiple_of((lax.rem(x + step, 4) * 2 + core) * 128, 128)
                outs[step][other] = result[pl.ds(row, 128), :]


def project(where, acts, pieces, moves, columns, absolute, before=()):
    any_space, vmem = pl.BlockSpec(memory_space=pl.ANY), pl.BlockSpec(memory_space=pltpu.VMEM)
    width = columns * 128
    if absolute:
        kept = sum(v.shape[2] for v in before)
        shapes = [jax.ShapeDtypeStruct((8, 128, kept + width), BF16)]
    else:
        shapes = [jax.ShapeDtypeStruct((2, 128, width), BF16)] * 4
    scratch = [
        pltpu.VMEM((4 * CH, width), BF16),
        pltpu.VMEM((2 * TOK, width), BF16),
        pltpu.SemaphoreType.DMA((len(moves),)),
    ]
    pinned = len(acts) == 1
    if pinned:
        acts = [pltpu.with_memory_space_constraint(acts[0], pltpu.VMEM)]
    else:
        shapes = shapes + [pltpu.VMEM((2, TOK, 4 * CH), BF16)]
        scratch.append(pltpu.SemaphoreType.DMA((2, 4)))
    act_specs = [vmem] if pinned else [any_space] * 8
    return pl.pallas_call(
        functools.partial(project_kernel, len(pieces), moves, absolute, pinned, len(before)),
        in_specs=[pl.BlockSpec(memory_space=pltpu.SMEM)] + act_specs + [any_space] * len(pieces) + [vmem] * len(before),
        out_specs=[vmem] * len(shapes),
        out_shape=shapes,
        scratch_shapes=scratch,
        compiler_params=pltpu.CompilerParams(vmem_limit_bytes=(40 if pinned else 52) << 20),
        cost_estimate=pl.CostEstimate(flops=2 * 1024 * 4096 * width, bytes_accessed=12 << 20, transcendentals=0),
    )(where, *acts, *pieces, *before)


def assemble_kernel(where_ref, *refs):
    out_ref = refs[-1]
    z, x, c = where_ref[1], where_ref[2], where_ref[3]

    def put(chip, core, columns, value):
        base = ((lax.rem(chip, 2) * 2 + core) * 2 + chip // 2) * 8
        for e, i in enumerate(columns):
            col = pl.multiple_of((base + lax.rem(z + i, 8)) * 128, 128)
            out_ref[:, pl.ds(col, 128)] = value[:, e * 128 : (e + 1) * 128]

    for chunk, columns in enumerate(CHUNKS[:-1]):
        parts = refs[chunk * 5 : chunk * 5 + 5]
        for step in range(4):
            chip = lax.rem(x + 4 - step, 4)
            put(chip, c, columns, parts[step][0])
            put(chip, 1 - c, columns, parts[4][step])
    for device in range(8):
        put(jnp.int32(device // 2), device % 2, CHUNKS[-1], refs[-2][device])


def assemble(where, parts):
    vmem = pl.BlockSpec(memory_space=pltpu.VMEM)
    return pl.pallas_call(
        assemble_kernel,
        in_specs=[pl.BlockSpec(memory_space=pltpu.SMEM)] + [vmem] * len(parts),
        out_specs=vmem,
        out_shape=jax.ShapeDtypeStruct((TOK // 4, 8 * CH), BF16),
        compiler_params=pltpu.CompilerParams(vmem_limit_bytes=24 << 20),
        cost_estimate=pl.CostEstimate(flops=0, bytes_accessed=4 << 20, transcendentals=0),
    )(where, *parts)


def shift(value, axis, steps):
    size = lax.axis_size(axis)
    return lax.ppermute(value, axis, [(i, (i + steps) % size) for i in range(size)])


def opposite(value, axis, size, first):
    pairs = [(2 * i + c, 2 * ((i + (first if c == 0 else -first)) % size) + c) for i in range(size) for c in range(2)]
    return lax.ppermute(value, (axis, "c") if isinstance(axis, str) else axis + ("c",), pairs)


def exchange(value, kind):
    held = [(d % 2) * 2 + (1 - d // 2 if kind else d // 2) for d in range(4)]
    pairs = [(a * 4 + b, held.index(b) * 4 + a) for a in range(4) for b in range(4)]
    return lax.ppermute(value, ("y", "xl", "c"), pairs)


def swap_cores(value):
    return lax.ppermute(value, "c", [(0, 1), (1, 0)])


def together(*values):
    return lax.optimization_barrier(values)


RING = ("xh", "xl")


def on_device(projected, short_taps, filter_taps, decay_rates, bypass_gain, out_weight):
    chip = lax.axis_index("xh") * 2 + lax.axis_index("xl")
    where = jnp.stack([lax.axis_index("y"), lax.axis_index("z"), chip, lax.axis_index("c")]).astype(jnp.int32)

    places = {i: [] for i in range(8)}
    buffers = []
    column = {}

    def keep_column(i, buffer):
        column[i] = buffer
        places[i] += [(len(buffers), 0, 0), (len(buffers), CH, 1)]
        buffers.append(buffer)

    def along_y(*columns):
        rows = [column[i][:CH] for i in columns]
        rows = rows[0] if len(rows) == 1 else jnp.concatenate(rows)
        return shift(rows, "y", -1), shift(rows, "y", 1)

    def keep_rows(columns, *both):
        for kind, buffer in zip((2, 3), both, strict=True):
            for e, i in enumerate(columns):
                places[i].append((len(buffers), e * CH, kind))
            buffers.append(buffer)

    def work_on(columns, acts, absolute, before=()):
        used, moves = [], []
        for col, i in enumerate(columns):
            for n, row, kind in places[i]:
                if n not in used:
                    used.append(n)
                moves.append((used.index(n), row, col, kind))
        return project(where, acts, [buffers[n] for n in used], tuple(moves), len(columns), absolute, before)

    def to_cell(sent):
        return [shift(sent[step], RING, step) for step in (1, 2, 3)]

    def other_cores(got):
        return swap_cores(jnp.stack([g[1] for g in got]))

    x = jnp.transpose(projected, (1, 0, 2))
    tail = tail_rows(x, short_taps)
    halo = lax.ppermute(tail, ("y", "xh", "z"), [(i, i + 1) for i in range(63)])
    blocks = [exchange(out_weight, 0), exchange(out_weight, 1)]
    gated = mixer(x, halo, short_taps, filter_taps, decay_rates, bypass_gain)
    *blocks, gated = together(*blocks, gated)
    keep_column(0, jnp.concatenate(blocks))
    one = opposite(gated, RING, 4, 1)
    first, last, *rows, one = together(shift(column[0], "z", -1), shift(column[0], "z", 1), *along_y(0), one)
    keep_column(1, first)
    keep_column(7, last)
    keep_rows((0,), *rows)
    two = opposite(together(gated, first)[0], RING, 4, -1)
    first, last, *rows, two = together(shift(column[1], "z", -1), shift(column[7], "z", 1), *along_y(1, 7), two)
    keep_column(2, first)
    keep_column(6, last)
    keep_rows((1, 7), *rows)
    three = opposite(together(one, first)[0], RING, 4, 1)
    first, last, *rows, three = together(shift(column[2], "z", -1), shift(column[6], "z", 1), *along_y(2, 6), three)
    keep_column(3, first)
    keep_column(5, last)
    keep_rows((2, 6), *rows)
    own, one, two, three, _ = together(gated, one, two, three, first)
    acts = [own, one, two, three] + [swap_cores(v) for v in (own, one, two, three)]
    *sent, held = work_on(CHUNKS[0], acts, False)
    middle, *rows = together(shift(column[3], "z", -1), *along_y(3, 5), *sent)
    rows, sent = rows[:2], rows[2:]
    keep_column(4, middle)
    keep_rows((3, 5), *rows)
    own_0, got_0 = sent[0], to_cell(sent)
    *rows, early = together(*along_y(4), *work_on(CHUNKS[1][:2], [held], True))
    keep_rows((4,), *rows)
    (last_sent,) = work_on(CHUNKS[1][2:], [held], True, [early])
    swapped_0 = other_cores([own_0] + got_0)
    last_got = lax.all_to_all(last_sent, RING + ("c",), 0, 0, tiled=True)
    return assemble(where, [own_0, *got_0, swapped_0, last_got])


def solution(mesh):
    fine = Mesh(mesh.devices.reshape(4, 2, 8, 2, 2), ("y", "xh", "z", "xl", "c"))
    ctx, tp = ("y", "xh", "z"), ("xl", "c")
    return jax.shard_map(
        on_device,
        mesh=fine,
        in_specs=(P(ctx, None, tp), P(None, None, tp), P(tp, None), P(tp), P(tp), P(tp, ctx)),
        out_specs=P(ctx + tp, None),
        check_vma=False,
    )
```

```python
import functools

import jax
import jax.numpy as jnp
import ml_dtypes
import numpy as np
from jax import lax
from jax.experimental import pallas as pl
from jax.experimental.pallas import tpu as pltpu
from jax.sharding import Mesh
from jax.sharding import PartitionSpec as P

TOK = 512
CH = 1024
TAPS = 128
WIN = 256
LANES = 256
CHUNKS = ((0, 1, 7, 2, 6), (3, 5, 4))
VMEM = 56 << 20
F32, BF16 = jnp.float32, jnp.bfloat16


def two_halves(matrix):
    high = matrix.astype(ml_dtypes.bfloat16)
    low = (matrix - high.astype(np.float64)).astype(ml_dtypes.bfloat16)
    return high, low


@functools.lru_cache(maxsize=None)
def transform_matrices():
    at = np.arange(WIN)
    half = WIN // 2
    angle = 2 * np.pi * (np.outer(np.arange(half), at) % WIN) / WIN
    sine = -np.sin(angle)
    sine[0] = np.cos(np.pi * at)
    forward = np.concatenate([np.cos(angle), sine])
    scale = np.where(np.arange(half) == 0, 1.0, 2.0)[:, None] / WIN
    scale_im = np.where(np.arange(half) == 0, 1.0, 2.0)[:, None] / WIN
    inverse = np.concatenate([np.cos(angle) * scale, sine * scale_im]).T[half:]
    fh, fl = two_halves(forward)
    ih, il = two_halves(inverse)
    return np.concatenate([fh, fl]), np.concatenate([ih, ih, il], axis=1)


def rolled(x, steps):
    return pltpu.roll(x, steps % x.shape[0], 0)


def featurize(rows, taps, count):
    lead = rows.shape[0] - count
    one = rolled(rows, 1)[lead:]
    two = rolled(rows, 2)[lead:]
    return (taps[0] * rows[lead:] + taps[1] * one + taps[2] * two).astype(BF16)


def tail_kernel(x_ref, before_ref, taps_ref, out_ref):
    streams = []
    raw = []
    for s in range(3):
        rows = x_ref[s].astype(F32)
        raw.append(rows[-8:])
        if s:
            taps = [taps_ref[j, s : s + 1, :] for j in range(3)]
            rows = jnp.concatenate([before_ref[s].astype(F32), rows], axis=0)
            streams.append(featurize(rows, taps, TAPS).astype(F32))
    out_ref[:TAPS, :] = (streams[0] * streams[1]).astype(BF16)
    row = lax.broadcasted_iota(jnp.int32, raw[0].shape, 0)
    packed = jnp.where(row < 2, rolled(raw[0], 2), jnp.where(row < 4, rolled(raw[1], 4), rolled(raw[2], 6)))
    out_ref[TAPS:, :] = jnp.concatenate([packed, jnp.zeros_like(packed)], axis=0).astype(BF16)


def tail_rows(x, taps):
    width = CH // 2
    return pl.pallas_call(
        tail_kernel,
        grid=(CH // width,),
        in_specs=[
            pl.BlockSpec((3, TAPS, width), lambda i: (0, TOK // TAPS - 1, i)),
            pl.BlockSpec((3, 16, width), lambda i: (0, (TOK - TAPS) // 16 - 1, i)),
            pl.BlockSpec((3, 3, width), lambda i: (0, 0, i)),
        ],
        out_specs=pl.BlockSpec((TAPS + 16, width), lambda i: (0, i)),
        out_shape=jax.ShapeDtypeStruct((TAPS + 16, CH), BF16),
        compiler_params=pltpu.CompilerParams(vmem_limit_bytes=VMEM),
        cost_estimate=pl.CostEstimate(flops=4 * TAPS * CH, bytes_accessed=2 << 20, transcendentals=0),
    )(x, x, taps)


def mixer_kernel(x_ref, halo_ref, taps_ref, filt_ref, rate_ref, gain_ref, fwd_ref, inv_ref, out_ref, prod, query):
    dot = functools.partial(lax.dot_general, preferred_element_type=F32)
    plain = (((1,), (0,)), ((), ()))
    half = WIN // 2

    lag = lax.broadcasted_iota(jnp.int32, (TAPS, LANES), 0).astype(F32)
    bank = (filt_ref[...].T * jnp.exp(-rate_ref[...] * lag)).astype(BF16)
    both = dot(fwd_ref[:, :half], bank, plain)
    spectrum = both[:WIN] + both[WIN:]
    h_re, h_im = spectrum[:half], spectrum[half:]
    first = lax.broadcasted_iota(jnp.int32, h_re.shape, 0) == 0
    h_last = jnp.where(first, h_im, h_re)
    h_im = jnp.where(first, 0.0, h_im)

    prod[:TAPS] = halo_ref[:TAPS]
    raw = halo_ref[TAPS:].astype(F32)[:8]
    for b in range(TOK // TAPS):
        made = []
        for s in range(3):
            taps = [taps_ref[j, s : s + 1, :] for j in range(3)]
            if b:
                rows = x_ref[s, b * TAPS - 16 : (b + 1) * TAPS, :].astype(F32)
            else:
                rows = jnp.concatenate([rolled(raw, 6 - 2 * s), x_ref[s, :TAPS, :].astype(F32)], axis=0)
            made.append(featurize(rows, taps, TAPS))
        query[b * TAPS : (b + 1) * TAPS] = made[0]
        prod[(b + 1) * TAPS : (b + 2) * TAPS] = (made[1].astype(F32) * made[2].astype(F32)).astype(BF16)

    for b in range(TOK // TAPS):
        both = dot(fwd_ref[...], prod[b * TAPS : b * TAPS + WIN], plain)
        spectrum = both[:WIN] + both[WIN:]
        re, im = spectrum[:half], spectrum[half:]
        y = jnp.concatenate([re * h_re - im * h_im, re * h_im + im * h_last], axis=0)
        high = y.astype(BF16)
        low = (y - high.astype(F32)).astype(BF16)
        long_part = dot(inv_ref[...], jnp.concatenate([high, low, high], axis=0), plain)
        here = prod[(b + 1) * TAPS : (b + 2) * TAPS].astype(F32)
        q = query[b * TAPS : (b + 1) * TAPS].astype(F32)
        out_ref[b * TAPS : (b + 1) * TAPS, :] = (q * (long_part + gain_ref[...] * here)).astype(BF16)


def mixer(x, halo, taps, filt, rate, gain):
    forward, inverse = transform_matrices()
    steps = CH // LANES
    return pl.pallas_call(
        mixer_kernel,
        grid=(steps,),
        in_specs=[
            pl.BlockSpec((3, TOK, LANES), lambda i: (0, 0, i)),
            pl.BlockSpec((TAPS + 16, LANES), lambda i: (0, i)),
            pl.BlockSpec((3, 3, LANES), lambda i: (0, 0, i)),
            pl.BlockSpec((LANES, TAPS), lambda i: (i, 0)),
            pl.BlockSpec((1, LANES), lambda i: (0, i)),
            pl.BlockSpec((1, LANES), lambda i: (0, i)),
            pl.BlockSpec(forward.shape, lambda i: (0, 0)),
            pl.BlockSpec(inverse.shape, lambda i: (0, 0)),
        ],
        out_specs=pl.BlockSpec((TOK, LANES), lambda i: (0, i)),
        out_shape=jax.ShapeDtypeStruct((TOK, CH), BF16),
        scratch_shapes=[
            pltpu.VMEM((TOK + TAPS, LANES), BF16),
            pltpu.VMEM((TOK, LANES), BF16),
        ],
        compiler_params=pltpu.CompilerParams(vmem_limit_bytes=VMEM),
        cost_estimate=pl.CostEstimate(flops=2 * 900 * 10**6, bytes_accessed=6 << 20, transcendentals=CH * TAPS),
    )(x, halo, taps, filt, rate[None, :], gain[None, :], jnp.asarray(forward), jnp.asarray(inverse))


def k_block(y, kind):
    if kind > 1:
        y = lax.rem(y + (1 if kind == 2 else 3), 4)
    return lax.rem(y, 2) * 2 + (1 - y // 2 if kind == 1 else y // 2)


def project_kernel(n_pieces, moves, absolute, pinned, n_before, where_ref, *refs):
    n_acts = 1 if pinned else 8
    act_refs, src, rest = refs[:n_acts], refs[n_acts : n_acts + n_pieces], refs[n_acts + n_pieces :]
    before, rest = rest[:n_before], rest[n_before:]
    n_out = 1 if absolute else 4
    outs, rest = rest[:n_out], rest[n_out:]
    if pinned:
        weight, result, sems = rest
        acts = act_refs[0]
    else:
        acts, weight, result, sems, act_sems = rest
    y, x, c = where_ref[0], where_ref[2], where_ref[3]
    act_copies = []
    for k in range(0 if pinned else 8):
        core = c if k < 4 else 1 - c
        chip = lax.rem(x + 4 + (0, 2 * core - 1, 1 - 2 * core, 2)[k % 4], 4)
        block = lax.rem(chip, 2) * 2 + core
        view = act_refs[k]
        target = acts.at[chip // 2, :, pl.ds(pl.multiple_of(block * CH, CH), CH)]
        act_copies.append(pltpu.make_async_copy(view, target, act_sems.at[chip // 2, block]))
    copies = []
    for n, (piece, row, col, kind) in enumerate(moves):
        start = pl.multiple_of(k_block(y, kind) * CH, CH)
        target = weight.at[pl.ds(start, CH), pl.ds(col * 128, 128)]
        copies.append(pltpu.make_async_copy(src[piece].at[pl.ds(row, CH)], target, sems.at[n]))
    ahead = [[], [], []]
    for copy, (piece, row, col, kind) in zip(copies, moves, strict=True):
        ahead[col // 2].append(copy)
    order = act_copies[0:1] + act_copies[4:5] + ahead[0] + act_copies[1:3] + act_copies[5:7] + ahead[1] + ahead[2]
    for copy in order + act_copies[3:4] + act_copies[7:8]:
        copy.start()
    columns = weight.shape[1]
    for turn in range(2):
        half = x // 2 if turn == 0 else 1 - x // 2
        for block in range(0 if pinned else 4):
            view = acts.at[half, :, pl.ds(block * CH, CH)]
            pltpu.make_async_copy(act_refs[0], view, act_sems.at[half, block]).wait()
        rows = pl.ds(pl.multiple_of(half * TOK, TOK), TOK)
        for p, at in enumerate(range(0, columns, 256)):
            if turn == 0:
                for copy in ahead[p]:
                    copy.wait()
            span = slice(at, min(at + 256, columns))
            result[rows, span] = jnp.dot(acts[half], weight[:, span], preferred_element_type=F32).astype(BF16)
    if absolute:
        kept = 0
        for ref in before:
            outs[0][:, :, : ref.shape[2]] = ref[...]
            kept = ref.shape[2]
        for device in range(8):
            outs[0][device, :, kept:] = result[device * 128 : (device + 1) * 128]
    else:
        for step in range(4):
            for other in range(2):
                core = c if other == 0 else 1 - c
                row = pl.multiple_of((lax.rem(x + step, 4) * 2 + core) * 128, 128)
                outs[step][other] = result[pl.ds(row, 128), :]


def project(where, acts, pieces, moves, columns, absolute, before=()):
    any_space, vmem = pl.BlockSpec(memory_space=pl.ANY), pl.BlockSpec(memory_space=pltpu.VMEM)
    width = columns * 128
    if absolute:
        kept = sum(v.shape[2] for v in before)
        shapes = [jax.ShapeDtypeStruct((8, 128, kept + width), BF16)]
    else:
        shapes = [jax.ShapeDtypeStruct((2, 128, width), BF16)] * 4
    scratch = [
        pltpu.VMEM((4 * CH, width), BF16),
        pltpu.VMEM((2 * TOK, width), BF16),
        pltpu.SemaphoreType.DMA((len(moves),)),
    ]
    pinned = len(acts) == 1
    if pinned:
        acts = [pltpu.with_memory_space_constraint(acts[0], pltpu.VMEM)]
    else:
        shapes = shapes + [pltpu.VMEM((2, TOK, 4 * CH), BF16)]
        scratch.append(pltpu.SemaphoreType.DMA((2, 4)))
    act_specs = [vmem] if pinned else [any_space] * 8
    return pl.pallas_call(
        functools.partial(project_kernel, len(pieces), moves, absolute, pinned, len(before)),
        in_specs=[pl.BlockSpec(memory_space=pltpu.SMEM)] + act_specs + [any_space] * len(pieces) + [vmem] * len(before),
        out_specs=[vmem] * len(shapes),
        out_shape=shapes,
        scratch_shapes=scratch,
        compiler_params=pltpu.CompilerParams(vmem_limit_bytes=(40 if pinned else 52) << 20),
        cost_estimate=pl.CostEstimate(flops=2 * 1024 * 4096 * width, bytes_accessed=12 << 20, transcendentals=0),
    )(where, *acts, *pieces, *before)


def assemble_kernel(where_ref, *refs):
    out_ref = refs[-1]
    z, x, c = where_ref[1], where_ref[2], where_ref[3]

    def put(chip, core, columns, value):
        base = ((lax.rem(chip, 2) * 2 + core) * 2 + chip // 2) * 8
        for e, i in enumerate(columns):
            col = pl.multiple_of((base + lax.rem(z + i, 8)) * 128, 128)
            out_ref[:, pl.ds(col, 128)] = value[:, e * 128 : (e + 1) * 128]

    for chunk, columns in enumerate(CHUNKS[:-1]):
        parts = refs[chunk * 5 : chunk * 5 + 5]
        for step in range(4):
            chip = lax.rem(x + 4 - step, 4)
            put(chip, c, columns, parts[step][0])
            put(chip, 1 - c, columns, parts[4][step])
    for device in range(8):
        put(jnp.int32(device // 2), device % 2, CHUNKS[-1], refs[-2][device])


def assemble(where, parts):
    vmem = pl.BlockSpec(memory_space=pltpu.VMEM)
    return pl.pallas_call(
        assemble_kernel,
        in_specs=[pl.BlockSpec(memory_space=pltpu.SMEM)] + [vmem] * len(parts),
        out_specs=vmem,
        out_shape=jax.ShapeDtypeStruct((TOK // 4, 8 * CH), BF16),
        compiler_params=pltpu.CompilerParams(vmem_limit_bytes=24 << 20),
        cost_estimate=pl.CostEstimate(flops=0, bytes_accessed=4 << 20, transcendentals=0),
    )(where, *parts)


def shift(value, axis, steps):
    size = lax.axis_size(axis)
    return lax.ppermute(value, axis, [(i, (i + steps) % size) for i in range(size)])


def opposite(value, axis, size, first):
    pairs = [(2 * i + c, 2 * ((i + (first if c == 0 else -first)) % size) + c) for i in range(size) for c in range(2)]
    return lax.ppermute(value, (axis, "c") if isinstance(axis, str) else axis + ("c",), pairs)


def exchange(value, kind):
    held = [(d % 2) * 2 + (1 - d // 2 if kind else d // 2) for d in range(4)]
    pairs = [(a * 4 + b, held.index(b) * 4 + a) for a in range(4) for b in range(4)]
    return lax.ppermute(value, ("y", "xl", "c"), pairs)


def swap_cores(value):
    return lax.ppermute(value, "c", [(0, 1), (1, 0)])


def together(*values):
    return lax.optimization_barrier(values)


RING = ("xh", "xl")


def on_device(projected, short_taps, filter_taps, decay_rates, bypass_gain, out_weight):
    chip = lax.axis_index("xh") * 2 + lax.axis_index("xl")
    where = jnp.stack([lax.axis_index("y"), lax.axis_index("z"), chip, lax.axis_index("c")]).astype(jnp.int32)

    places = {i: [] for i in range(8)}
    buffers = []
    column = {}

    def keep_column(i, buffer):
        column[i] = buffer
        places[i] += [(len(buffers), 0, 0), (len(buffers), CH, 1)]
        buffers.append(buffer)

    def along_y(*columns):
        rows = [column[i][:CH] for i in columns]
        rows = rows[0] if len(rows) == 1 else jnp.concatenate(rows)
        return shift(rows, "y", -1), shift(rows, "y", 1)

    def keep_rows(columns, *both):
        for kind, buffer in zip((2, 3), both, strict=True):
            for e, i in enumerate(columns):
                places[i].append((len(buffers), e * CH, kind))
            buffers.append(buffer)

    def work_on(columns, acts, absolute, before=()):
        used, moves = [], []
        for col, i in enumerate(columns):
            for n, row, kind in places[i]:
                if n not in used:
                    used.append(n)
                moves.append((used.index(n), row, col, kind))
        return project(where, acts, [buffers[n] for n in used], tuple(moves), len(columns), absolute, before)

    def to_cell(sent):
        return [shift(sent[step], RING, step) for step in (1, 2, 3)]

    def other_cores(got):
        return swap_cores(jnp.stack([g[1] for g in got]))

    x = jnp.transpose(projected, (1, 0, 2))
    tail = tail_rows(x, short_taps)
    halo = lax.ppermute(tail, ("y", "xh", "z"), [(i, i + 1) for i in range(63)])
    blocks = [exchange(out_weight, 0), exchange(out_weight, 1)]
    gated = mixer(x, halo, short_taps, filter_taps, decay_rates, bypass_gain)
    *blocks, gated = together(*blocks, gated)
    keep_column(0, jnp.concatenate(blocks))
    one = opposite(gated, RING, 4, 1)
    first, last, *rows, one = together(shift(column[0], "z", -1), shift(column[0], "z", 1), *along_y(0), one)
    keep_column(1, first)
    keep_column(7, last)
    keep_rows((0,), *rows)
    two = opposite(together(gated, first)[0], RING, 4, -1)
    first, last, *rows, two = together(shift(column[1], "z", -1), shift(column[7], "z", 1), *along_y(1, 7), two)
    keep_column(2, first)
    keep_column(6, last)
    keep_rows((1, 7), *rows)
    three = opposite(together(one, first)[0], RING, 4, 1)
    first, last, *rows, three = together(shift(column[2], "z", -1), shift(column[6], "z", 1), *along_y(2, 6), three)
    keep_column(3, first)
    keep_column(5, last)
    keep_rows((2, 6), *rows)
    own, one, two, three, _ = together(gated, one, two, three, first)
    acts = [own, one, two, three] + [swap_cores(v) for v in (own, one, two, three)]
    *sent, held = work_on(CHUNKS[0], acts, False)
    middle, *rows = together(shift(column[3], "z", -1), *along_y(3, 5), *sent)
    rows, sent = rows[:2], rows[2:]
    keep_column(4, middle)
    keep_rows((3, 5), *rows)
    own_0, got_0 = sent[0], to_cell(sent)
    *rows, early = together(*along_y(4), *work_on(CHUNKS[1][:2], [held], True))
    keep_rows((4,), *rows)
    (last_sent,) = work_on(CHUNKS[1][2:], [held], True, [early])
    swapped_0 = other_cores([own_0] + got_0)
    last_got = lax.all_to_all(last_sent, RING + ("c",), 0, 0, tiled=True)
    return assemble(where, [own_0, *got_0, swapped_0, last_got])


def solution(mesh):
    fine = Mesh(mesh.devices.reshape(4, 2, 8, 2, 2), ("y", "xh", "z", "xl", "c"))
    ctx, tp = ("y", "xh", "z"), ("xl", "c")
    return jax.shard_map(
        on_device,
        mesh=fine,
        in_specs=(P(ctx, None, tp), P(None, None, tp), P(tp, None), P(tp), P(tp), P(tp, ctx)),
        out_specs=P(ctx + tp, None),
        check_vma=False,
    )
```
